512 devices in a mesh: section: 8 (over z_hi, core), expert: 64 (over z_lo, x, y).
Axes of the slice: x: 4, y: 8, z: 8 (z_hi: 4, z_lo: 2; z = z_hi * 2 + z_lo), core: 2. Of those that a mesh axis runs over, the one named last changes fastest.
Arguments:
- tokens_forward: bfloat16 [8, 2560, 2048], P('section', 'expert'), may hold values from -6 to 6
- tokens_reverse: bfloat16 [8, 2560, 2048], P('section', 'expert'), may hold values from -6 to 6
- routes_forward: int32 [8, 2560, 8], P('section', 'expert'), may hold values from 0 to 63, all different within a row; in each aligned block of 40 rows (0 to 39, 40 to 79, ..., all dimensions but the last counted through in order) at most 7 rows name the same one
- routes_reverse: int32 [8, 2560, 8], P('section', 'expert'), may hold values from 0 to 63, all different within a row; in each aligned block of 40 rows (0 to 39, 40 to 79, ..., all dimensions but the last counted through in order) at most 7 rows name the same one
- hidden_forward: bfloat16 [8, 64, 448, 768], P('section', 'expert'), may hold values from -6 to 6
- hidden_reverse: bfloat16 [8, 64, 448, 768], P('section', 'expert'), may hold values from -6 to 6
- router_weight: bfloat16 [8, 2048, 64], P('section'), may hold values from -0.125 to 0.125
- down_weight: bfloat16 [8, 64, 768, 2048], P('section', 'expert'), may hold values from -0.21875 to 0.21875
Outputs:
- arrived_forward: bfloat16 [8, 2560, 2048], P('section', 'expert')
- arrived_reverse: bfloat16 [8, 2560, 2048], P('section', 'expert')
The draws below stay inside these ranges and needn't reach their ends.
Inputs may be any that keep to these rules, and one draw needn't show every extreme that they name: `routes_forward`: the 8 experts of a token differ. The 40 tokens of one device (aligned blocks of rows at one section) name no expert more than 7 times in all, and in some device's tokens an expert is named exactly 7 times. `routes_reverse`: as for routes_forward.
All inputs are finite; a program needn't handle non-finite values.
Results may differ from the reference program's by a relative error of at most 0.0029.
Values may be sent and summed in bfloat16 or wider, within the bound.
No kernel may reach another device: no remote copies, remote signals or barrier semaphores. Data moves between devices by JAX's collectives and lax.ppermute only.
A program may use at most 64 MiB of HBM per device.

```python
import math
import jax
import jax.numpy as jnp
import numpy as np
from jax import lax

D = 2048
H = 768
TOP = 8
TOK_DEV = 40
EXPERTS = 64
CAP = 7
TOKENS = 2560
N_SECTION = 8
N_EXPERT = 64


def block_scale(own_key, extent, pieces, least, top_value):
    loudness, own = 1.0, jax.random.fold_in(own_key, 6)
    for axis_at, parts in pieces:
        steps = jnp.exp(jax.random.uniform(jax.random.fold_in(own, axis_at), (parts,), jnp.float32, least / len(pieces), top_value / len(pieces)))
        loudness = loudness * jnp.repeat(steps, extent[axis_at] // parts).reshape([-1 if axis == axis_at else 1 for axis in range(len(extent))])
    return loudness


def routed_block(key, own, number, rows, number_of, top, bound, slope):
    sequence = jax.random.permutation(key, number_of)
    heavy_load, usual = shares(number_of, rows * top, bound, slope, True), shares(number_of, rows * top, bound, slope, False)
    places = jnp.arange(number_of)

    def named(lengths, offset_by):
        used = int((lengths > 0).sum())
        fixed = max(1, used // 4)
        shifted = fixed + (places - fixed + offset_by * (used - fixed)) % max(1, number_of - fixed)
        return jnp.zeros((number_of,), jnp.int32).at[sequence[jnp.where(places < fixed, places, shifted)]].set(jnp.asarray(lengths, jnp.int32))

    lengths = jnp.where(number % 4 == 0, named(heavy_load, number // 4), named(usual, number - number // 4 - 1))
    mixed = jax.random.permutation(jax.random.fold_in(own, 3), number_of)
    source_of, receiver = mixed[0:number_of // 2 * 2:2], mixed[1:number_of // 2 * 2:2]
    margin = jnp.minimum(lengths[source_of] - 1, bound - lengths[receiver]) // 2
    margin = jnp.where((source_of == sequence[0]) | (receiver == sequence[0]) | (lengths[receiver] == 0), 0, jnp.maximum(margin, 0))
    shifted = jax.random.randint(jax.random.fold_in(own, 4), (number_of // 2,), 0, 1 << 20) % (margin + 1)
    lengths = lengths.at[source_of].add(-shifted).at[receiver].add(shifted)
    labels = jnp.searchsorted(jnp.cumsum(lengths), jnp.arange(rows * top), side="right").astype(jnp.int32)
    listing = labels.reshape(top, rows).T
    listing = listing[jax.random.permutation(jax.random.fold_in(own, 1), rows)]
    offset_by = jax.random.randint(jax.random.fold_in(own, 2), (rows, 1), 0, top)
    return jnp.take_along_axis(listing, (jnp.arange(top)[None, :] + offset_by) % top, axis=1)


def shares(count, total, limit, skew, full):
    portions = [(1 << 20) // math.isqrt(grade ** skew) + 1 for grade in range(1, count + 1)]
    largest = limit if full else min(limit, max(-(-total // count), total * portions[0] // sum(portions)))
    least = 1 if total - largest >= count - 1 else 0
    holding, rest = [largest] + [least] * (count - 1), total - largest - least * (count - 1)
    while rest > 0:
        movable = [i for i in range(1, count) if holding[i] < largest] or [i for i in range(1, count) if holding[i] < limit]
        pool, budget = sum([portions[i] for i in movable]), rest
        for i in movable:
            addition = min(limit - holding[i], max(1, budget * portions[i] // pool), rest)
            holding[i] = holding[i] + addition
            rest = rest - addition
    return np.array(holding)


def normal_values(rng, shape, deviation, reach, pieces=(), held_as=jnp.bfloat16):
    result = jax.random.normal(rng, shape, jnp.float32) * deviation
    if len(pieces) > 0:
        result = block_scale(rng, shape, pieces, -0.22, 0.18) * result
    return jnp.clip(result, min=-reach, max=reach).astype(held_as)


def setup_inputs(seed: int = 0) -> dict:
    keys = jax.random.split(jax.random.key(seed), 9)
    tokens_forward = normal_values(keys[0], (N_SECTION, TOKENS, D), 1.0, 6.0, ((0, 8), (1, 64)))
    tokens_reverse = normal_values(keys[1], (N_SECTION, TOKENS, D), 1.0, 6.0, ((0, 8), (1, 64)))
    routes_forward_keys = jax.random.split(jax.random.fold_in(keys[2], 1), N_SECTION * TOKENS // TOK_DEV)
    routes_forward_turns = jax.random.permutation(jax.random.fold_in(keys[2], 3), N_SECTION * TOKENS // TOK_DEV)
    routes_forward = jax.vmap(lambda own, number: routed_block(jax.random.fold_in(keys[2], 2), own, number, TOK_DEV, EXPERTS, TOP, CAP, 2))(routes_forward_keys, routes_forward_turns).reshape((N_SECTION, TOKENS, TOP))
    routes_reverse_keys = jax.random.split(jax.random.fold_in(keys[3], 1), N_SECTION * TOKENS // TOK_DEV)
    routes_reverse_turns = jax.random.permutation(jax.random.fold_in(keys[3], 3), N_SECTION * TOKENS // TOK_DEV)
    routes_reverse = jax.vmap(lambda own, number: routed_block(jax.random.fold_in(keys[3], 2), own, number, TOK_DEV, EXPERTS, TOP, CAP, 2))(routes_reverse_keys, routes_reverse_turns).reshape((N_SECTION, TOKENS, TOP))
    hidden_forward = normal_values(keys[4], (N_SECTION, EXPERTS, EXPERTS * CAP, H), 1.0, 6.0, ((0, 8), (1, 64)))
    hidden_reverse = normal_values(keys[5], (N_SECTION, EXPERTS, EXPERTS * CAP, H), 1.0, 6.0, ((0, 8), (1, 64)))
    router_weight = normal_values(keys[6], (N_SECTION, D, EXPERTS), D ** -0.5, 0.125, ((0, 8),))
    down_weight = normal_values(keys[7], (N_SECTION, EXPERTS, H, D), H ** -0.5, 0.21875, ((0, 8), (1, 64)))
    return dict(tokens_forward=tokens_forward, tokens_reverse=tokens_reverse, routes_forward=routes_forward, routes_reverse=routes_reverse, hidden_forward=hidden_forward, hidden_reverse=hidden_reverse, router_weight=router_weight, down_weight=down_weight)


def expert_product(pair):
    rows, weight = pair
    return jnp.dot(rows, weight, preferred_element_type=jnp.float32).astype(jnp.bfloat16)


def moe_layer(tokens, routes, hidden, router, down_w):
    logits = jnp.dot(tokens, router, preferred_element_type=jnp.float32)
    chosen = jnp.take_along_axis(logits, routes, axis=1)
    raised = jnp.exp(chosen)
    gate_share = raised / jnp.sum(raised, axis=1, keepdims=True)
    block_ids = routes.reshape(N_EXPERT, TOK_DEV * TOP).astype(jnp.int32)
    one_hot = (block_ids[:, :, None] == jnp.arange(EXPERTS, dtype=jnp.int32)[None, None, :]).astype(jnp.int32)
    slot_rank = jnp.sum((jnp.cumsum(one_hot, axis=1) - one_hot) * one_hot, axis=2).astype(jnp.int32)
    column = (jnp.arange(N_EXPERT, dtype=jnp.int32)[:, None] * CAP + slot_rank).astype(jnp.int32)
    expert_out = lax.map(expert_product, (hidden, down_w))
    picked = expert_out[block_ids.reshape(-1), column.reshape(-1)].reshape(TOKENS, TOP, D)
    combined = jnp.sum(gate_share[:, :, None] * picked.astype(jnp.float32), axis=1)
    return (tokens.astype(jnp.float32) + combined).astype(jnp.bfloat16)


def reference(tokens_forward, tokens_reverse, routes_forward, routes_reverse, hidden_forward, hidden_reverse, router_weight, down_weight):
    def per_section(items):
        rising, falling, rising_routes, falling_routes, rising_hidden, falling_hidden, router, down_w = items
        return (moe_layer(rising, rising_routes, rising_hidden, router, down_w), moe_layer(falling, falling_routes, falling_hidden, router, down_w))

    rising_out, falling_out = lax.map(per_section, (tokens_forward, tokens_reverse, routes_forward, routes_reverse, hidden_forward, hidden_reverse, router_weight, down_weight))
    return jnp.roll(rising_out, 1, axis=0), jnp.roll(falling_out, -1, axis=0)
```

```python
import functools

import jax
import jax.numpy as jnp
from jax import lax
from jax.experimental import pallas as pl
from jax.experimental.pallas import tpu as pltpu
from jax.sharding import Mesh
from jax.sharding import PartitionSpec as P

TOK = 40
CAP = 7
EXPERTS = 64
NY = 8
ROWS = EXPERTS * CAP
STEP = 512
ORDER = (3, 1, 4, -3, -1, 2, -2, 0)
VMEM = pl.BlockSpec(memory_space=pltpu.VMEM)
F32 = jnp.float32
BF16 = jnp.bfloat16
MIRROR = False


def gate_kernel(tf_ref, tr_ref, rf_ref, rr_ref, router_ref, own_ref, far_ref, m1_ref, m2_ref, m3_ref, table):
    experts = lax.broadcasted_iota(jnp.int32, (EXPERTS, TOK), 0)
    later = lax.broadcasted_iota(jnp.int32, (TOK, TOK), 0) < lax.broadcasted_iota(jnp.int32, (TOK, TOK), 1)
    later = later.astype(F32).astype(BF16)
    shares, ranks = [], []
    for t_ref, r_ref in ((tf_ref, rf_ref), (tr_ref, rr_ref)):
        logits = lax.dot_general(
            router_ref[...], t_ref[...], (((1,), (1,)), ((), ())), preferred_element_type=F32
        )
        named = jnp.zeros((EXPERTS, TOK), F32)
        for k in range(8):
            named = named + (r_ref[k : k + 1, :] == experts).astype(F32)
        raised = jnp.where(named > 0, jnp.exp(logits), 0.0)
        shares.append(raised / jnp.sum(raised, axis=0, keepdims=True))
        rank = jnp.dot(named.astype(BF16), later, preferred_element_type=F32)
        ranks.append(jnp.where(named > 0, rank, -1.0))
    pad = jnp.zeros((EXPERTS, 128 - 2 * TOK), F32)
    table[:EXPERTS] = jnp.concatenate([*shares, pad], axis=1)
    table[EXPERTS:] = jnp.concatenate([*ranks, pad], axis=1)

    def part(ref, at, offset):
        place = lax.rem(lax.axis_index("y").astype(jnp.int32) + offset, NY)
        ref[at : at + 8] = table[pl.ds(place, 8, stride=NY), :]
        ref[at + 8 : at + 16] = table[pl.ds(EXPERTS + place, 8, stride=NY), :]

    part(own_ref, 0, 0)
    part(far_ref, 0, 4)
    for offset, ref in ((1, m1_ref), (2, m2_ref), (3, m3_ref)):
        part(ref, 0, offset)
        part(ref, 16, offset + 4)


def gate_tables(tf, tr, rf, rr, router_t):
    return pl.pallas_call(
        gate_kernel,
        out_shape=[jax.ShapeDtypeStruct((size, 128), F32) for size in (16, 16, 32, 32, 32)],
        in_specs=[VMEM] * 5,
        out_specs=[VMEM] * 5,
        scratch_shapes=[pltpu.VMEM((2 * EXPERTS, 128), F32)],
        cost_estimate=pl.CostEstimate(flops=2 * 80 * 2048 * 64, bytes_accessed=700_000, transcendentals=5120),
    )(tf, tr, rf, rr, router_t)


def combine_kernel(m, own_ref, m1_ref, m2_ref, m3_ref, far_ref, rows_ref, *outs_and_scratch):
    *outs, wide, weights = outs_and_scratch

    @pl.when(pl.program_id(0) == 0)
    def _():
        y = lax.axis_index("y").astype(jnp.int32)
        turn = 1 - 2 * lax.rem(lax.axis_index("section").astype(jnp.int32), 2) if MIRROR else 1
        column = lax.broadcasted_iota(jnp.int32, (1, ROWS), 1)
        zx = sum((column >= NY * CAP * i).astype(jnp.int32) for i in range(1, EXPERTS // NY))
        column = column - NY * CAP * zx
        dest = sum((column >= CAP * i).astype(jnp.int32) for i in range(1, NY))
        slot = (column - CAP * dest).astype(F32)
        tables = jnp.concatenate([own_ref[...], m1_ref[:16], m2_ref[:16], m3_ref[:16], far_ref[...]], axis=0)
        by_token = tables.T[m * TOK : (m + 1) * TOK]
        high = by_token.astype(BF16)
        low = (by_token - high.astype(F32)).astype(BF16)
        behind = (y + NY - dest) & (NY - 1)
        place = lax.broadcasted_iota(jnp.int32, (128, ROWS), 0)
        of_share = (place == behind * 16 + zx).astype(F32).astype(BF16)
        of_rank = (place == behind * 16 + zx + 8).astype(F32).astype(BF16)
        share = jnp.dot(jnp.concatenate([high, low], axis=0), of_share, preferred_element_type=F32)
        mine = jnp.dot(high, of_rank, preferred_element_type=F32) == slot
        share_high = jnp.where(mine, share[:TOK], 0.0)
        share_low = jnp.where(mine, share[TOK:], 0.0)
        for i, k in enumerate(ORDER):
            there = dest == lax.rem(y + NY + turn * k, NY)
            wide[i * TOK : (i + 1) * TOK] = jnp.where(there, share_high, 0.0)
            wide[(NY + i) * TOK : (NY + i + 1) * TOK] = jnp.where(there, share_low, 0.0)
        weights[...] = wide[...].astype(BF16)

    total = jnp.dot(weights[...], rows_ref[...], preferred_element_type=F32)
    summed = (total[: NY * TOK] + total[NY * TOK :]).astype(BF16)
    at = 0
    for out in outs:
        out[...] = summed[at : at + out.shape[0]]
        at += out.shape[0]


def combine(m, tables, rows):
    width = rows.shape[1]
    sizes = (2 * TOK, TOK, 2 * TOK, 3 * TOK)
    whole = lambda shape: pl.BlockSpec(shape, lambda i: (0,) * len(shape))
    return pl.pallas_call(
        functools.partial(combine_kernel, m),
        grid=(width // STEP,),
        out_shape=[jax.ShapeDtypeStruct((size, width), BF16) for size in sizes],
        in_specs=[
            *[whole(table.shape) for table in tables],
            pl.BlockSpec((ROWS, STEP), lambda i: (0, i)),
        ],
        out_specs=[pl.BlockSpec((size, STEP), lambda i: (0, i)) for size in sizes],
        scratch_shapes=[pltpu.VMEM((2 * NY * TOK, ROWS), F32), pltpu.VMEM((2 * NY * TOK, ROWS), BF16)],
        compiler_params=pltpu.CompilerParams(vmem_limit_bytes=32 * 1024 * 1024),
        cost_estimate=pl.CostEstimate(
            flops=4 * NY * TOK * ROWS * width, bytes_accessed=2 * (ROWS + NY * TOK) * width, transcendentals=0
        ),
    )(*tables, rows)


def passed_along(block, axis, distance):
    size = lax.axis_size(axis)
    return lax.ppermute(block, axis, [(i, (i + distance) % size) for i in range(size)])


def onward(block, distance):
    if not MIRROR:
        return passed_along(block, "y", distance)
    ns = lax.axis_size("section")
    route = [
        (s * NY + i, s * NY + (i + (distance if s % 2 == 0 else -distance)) % NY) for s in range(ns) for i in range(NY)
    ]
    return lax.ppermute(block, ("section", "y"), route)


def add(*terms):
    total = terms[0].astype(F32)
    for term in terms[1:]:
        total = total + term.astype(F32)
    return total.astype(BF16)


def shards(tf, tr, rf, rr, hf, hr, router, down):
    tokens = (tf[0], tr[0])
    own, far, *sent = gate_tables(tf[0], tr[0], rf[0].T, rr[0].T, router[0].T)
    hf, *sent = lax.optimization_barrier((hf, *sent))
    near = [passed_along(block, "y", 1 + i) for i, block in enumerate(sent)]
    far = passed_along(jnp.concatenate([far] + [block[16:] for block in near]), "y", 4)
    down_w = down[0, 0]
    arrived = []
    for m, hidden in enumerate((hf, hr)):
        rows = jnp.dot(hidden[0, 0], down_w, preferred_element_type=F32).astype(BF16)
        if m == 1:
            rows, far = lax.optimization_barrier((rows, far))
        back = lax.all_to_all(rows, ("zl", "x"), split_axis=0, concat_axis=0, tiled=True)
        ahead31, ahead4, behind31, kept = combine(m, (own, *near, far), back)
        got_ahead = onward(ahead31, 1)
        got_four = onward(ahead4, 2)
        got_behind = onward(behind31, -1)
        last_ahead = onward(add(kept[:TOK], got_ahead[:TOK], got_four), 2)
        last_behind = onward(add(kept[TOK : 2 * TOK], got_behind[:TOK]), -2)
        layer = add(tokens[m], kept[2 * TOK :], got_ahead[TOK:], got_behind[TOK:], last_ahead, last_behind)
        arrived.append(passed_along(layer, "section", 1 - 2 * m)[None])
    return tuple(arrived)


def solution(mesh):
    fine = Mesh(mesh.devices.reshape(8, 2, 4, NY), ("section", "zl", "x", "y"))
    expert = ("zl", "x", "y")
    row = P("section", expert, None)
    block = P("section", expert, None, None)
    return jax.shard_map(
        shards,
        mesh=fine,
        in_specs=(row, row, row, row, block, block, P("section", None, None), block),
        out_specs=(row, row),
        check_vma=False,
    )
```

```python
import functools

import jax
import jax.numpy as jnp
from jax import lax
from jax.experimental import pallas as pl
from jax.experimental.pallas import tpu as pltpu
from jax.sharding import Mesh
from jax.sharding import PartitionSpec as P

TOK = 40
CAP = 7
EXPERTS = 64
NY = 8
ROWS = EXPERTS * CAP
STEP = 512
ORDER = (3, 1, 4, -3, -1, 2, -2, 0)
VMEM = pl.BlockSpec(memory_space=pltpu.VMEM)
F32 = jnp.float32
BF16 = jnp.bfloat16


def gate_kernel(tf_ref, tr_ref, rf_ref, rr_ref, router_ref, own_ref, far_ref, m1_ref, m2_ref, m3_ref, table):
    experts = lax.broadcasted_iota(jnp.int32, (EXPERTS, TOK), 0)
    later = lax.broadcasted_iota(jnp.int32, (TOK, TOK), 0) < lax.broadcasted_iota(jnp.int32, (TOK, TOK), 1)
    later = later.astype(F32).astype(BF16)
    shares, ranks = [], []
    for t_ref, r_ref in ((tf_ref, rf_ref), (tr_ref, rr_ref)):
        logits = lax.dot_general(
            router_ref[...], t_ref[...], (((1,), (1,)), ((), ())), preferred_element_type=F32
        )
        named = jnp.zeros((EXPERTS, TOK), F32)
        for k in range(8):
            named = named + (r_ref[k : k + 1, :] == experts).astype(F32)
        raised = jnp.where(named > 0, jnp.exp(logits), 0.0)
        shares.append(raised / jnp.sum(raised, axis=0, keepdims=True))
        rank = jnp.dot(named.astype(BF16), later, preferred_element_type=F32)
        ranks.append(jnp.where(named > 0, rank, -1.0))
    pad = jnp.zeros((EXPERTS, 128 - 2 * TOK), F32)
    table[:EXPERTS] = jnp.concatenate([*shares, pad], axis=1)
    table[EXPERTS:] = jnp.concatenate([*ranks, pad], axis=1)

    def part(ref, at, offset):
        place = lax.rem(lax.axis_index("y").astype(jnp.int32) + offset, NY)
        ref[at : at + 8] = table[pl.ds(place, 8, stride=NY), :]
        ref[at + 8 : at + 16] = table[pl.ds(EXPERTS + place, 8, stride=NY), :]

    part(own_ref, 0, 0)
    part(far_ref, 0, 4)
    for offset, ref in ((1, m1_ref), (2, m2_ref), (3, m3_ref)):
        part(ref, 0, offset)
        part(ref, 16, offset + 4)


def gate_tables(tf, tr, rf, rr, router_t):
    return pl.pallas_call(
        gate_kernel,
        out_shape=[jax.ShapeDtypeStruct((size, 128), F32) for size in (16, 16, 32, 32, 32)],
        in_specs=[VMEM] * 5,
        out_specs=[VMEM] * 5,
        scratch_shapes=[pltpu.VMEM((2 * EXPERTS, 128), F32)],
        cost_estimate=pl.CostEstimate(flops=2 * 80 * 2048 * 64, bytes_accessed=700_000, transcendentals=5120),
    )(tf, tr, rf, rr, router_t)


def combine_kernel(m, held_ref, m1_ref, m2_ref, m3_ref, far_ref, rows_ref, *outs_and_scratch):
    *outs, wide, weights = outs_and_scratch

    @pl.when(pl.program_id(0) == 0)
    def _():
        y = lax.axis_index("y").astype(jnp.int32)
        column = lax.broadcasted_iota(jnp.int32, (1, ROWS), 1)
        zx = sum((column >= NY * CAP * i).astype(jnp.int32) for i in range(1, EXPERTS // NY))
        column = column - NY * CAP * zx
        dest = sum((column >= CAP * i).astype(jnp.int32) for i in range(1, NY))
        slot = (column - CAP * dest).astype(F32)
        tables = jnp.concatenate([held_ref[64:], m1_ref[:16], m2_ref[:16], m3_ref[:16], far_ref[:64]], axis=0)
        by_token = tables.T[m * TOK : (m + 1) * TOK]
        high = by_token.astype(BF16)
        low = (by_token - high.astype(F32)).astype(BF16)
        behind = (y + NY - dest) & (NY - 1)
        place = lax.broadcasted_iota(jnp.int32, (128, ROWS), 0)
        of_share = (place == behind * 16 + zx).astype(F32).astype(BF16)
        of_rank = (place == behind * 16 + zx + 8).astype(F32).astype(BF16)
        share = jnp.dot(jnp.concatenate([high, low], axis=0), of_share, preferred_element_type=F32)
        mine = jnp.dot(high, of_rank, preferred_element_type=F32) == slot
        share_high = jnp.where(mine, share[:TOK], 0.0)
        share_low = jnp.where(mine, share[TOK:], 0.0)
        for i, k in enumerate(ORDER):
            there = dest == lax.rem(y + NY + k, NY)
            wide[i * TOK : (i + 1) * TOK] = jnp.where(there, share_high, 0.0)
            wide[(NY + i) * TOK : (NY + i + 1) * TOK] = jnp.where(there, share_low, 0.0)
        weights[...] = wide[...].astype(BF16)

    total = jnp.dot(weights[...], rows_ref[...], preferred_element_type=F32)
    summed = (total[: NY * TOK] + total[NY * TOK :]).astype(BF16)
    at = 0
    for out in outs:
        out[...] = summed[at : at + out.shape[0]]
        at += out.shape[0]


def combine(m, tables, rows):
    width = rows.shape[1]
    sizes = (2 * TOK, TOK, 2 * TOK, 3 * TOK)
    whole = lambda shape: pl.BlockSpec(shape, lambda i: (0,) * len(shape))
    return pl.pallas_call(
        functools.partial(combine_kernel, m),
        grid=(width // STEP,),
        out_shape=[jax.ShapeDtypeStruct((size, width), BF16) for size in sizes],
        in_specs=[
            *[whole(table.shape) for table in tables],
            pl.BlockSpec((ROWS, STEP), lambda i: (0, i)),
        ],
        out_specs=[pl.BlockSpec((size, STEP), lambda i: (0, i)) for size in sizes],
        scratch_shapes=[pltpu.VMEM((2 * NY * TOK, ROWS), F32), pltpu.VMEM((2 * NY * TOK, ROWS), BF16)],
        compiler_params=pltpu.CompilerParams(vmem_limit_bytes=32 * 1024 * 1024),
        cost_estimate=pl.CostEstimate(
            flops=4 * NY * TOK * ROWS * width, bytes_accessed=2 * (ROWS + NY * TOK) * width, transcendentals=0
        ),
    )(*tables, rows)


def passed_along(block, axis, distance):
    size = lax.axis_size(axis)
    return lax.ppermute(block, axis, [(i, (i + distance) % size) for i in range(size)])


def halfway(block):
    ns = lax.axis_size("section")
    route = [(s * NY + i, s * NY + (i + (2 if s % 2 == 0 else -2)) % NY) for s in range(ns) for i in range(NY)]
    return lax.ppermute(block, ("section", "y"), route)


def add(*terms):
    total = terms[0].astype(F32)
    for term in terms[1:]:
        total = total + term.astype(F32)
    return total.astype(BF16)


def shards(tf, tr, rf, rr, hf, hr, router, down):
    tokens = (tf[0], tr[0])
    up = lax.axis_index("section") % 2 == 0
    own, far, *sent = gate_tables(tf[0], tr[0], rf[0].T, rr[0].T, router[0].T)
    hf, *sent = lax.optimization_barrier((hf, *sent))
    near = [passed_along(block, "y", 1 + i) for i, block in enumerate(sent)]
    held = jnp.concatenate([far] + [block[16:] for block in near] + [own])
    far = passed_along(held, "y", 4)
    down_w = down[0, 0]
    arrived = []
    for m, hidden in enumerate((hf, hr)):
        rows = jnp.dot(hidden[0, 0], down_w, preferred_element_type=F32).astype(BF16)
        if m == 1:
            rows, far = lax.optimization_barrier((rows, far))
        back = lax.all_to_all(rows, ("zl", "x"), split_axis=0, concat_axis=0, tiled=True)
        ahead31, ahead4, behind31, kept = combine(m, (held, *near, far), back)
        got_ahead = passed_along(ahead31, "y", 1)
        got_four = halfway(ahead4)
        got_behind = passed_along(behind31, "y", -1)
        last_ahead = add(kept[:TOK], got_ahead[:TOK], jnp.where(up, got_four, 0))
        last_behind = add(kept[TOK : 2 * TOK], got_behind[:TOK], jnp.where(up, 0, got_four))
        last_ahead = passed_along(last_ahead, "y", 2)
        last_behind = passed_along(last_behind, "y", -2)
        layer = add(tokens[m], kept[2 * TOK :], got_ahead[TOK:], got_behind[TOK:], last_ahead, last_behind)
        arrived.append(passed_along(layer, "section", 1 - 2 * m)[None])
    return tuple(arrived)


def solution(mesh):
    fine = Mesh(mesh.devices.reshape(8, 2, 4, NY), ("section", "zl", "x", "y"))
    expert = ("zl", "x", "y")
    row = P("section", expert, None)
    block = P("section", expert, None, None)
    return jax.shard_map(
        shards,
        mesh=fine,
        in_specs=(row, row, row, row, block, block, P("section", None, None), block),
        out_specs=(row, row),
        check_vma=False,
    )
```

```python
import functools

import jax
import jax.numpy as jnp
from jax import lax
from jax.experimental import pallas as pl
from jax.experimental.pallas import tpu as pltpu
from jax.sharding import Mesh
from jax.sharding import PartitionSpec as P

TOK = 40
CAP = 7
EXPERTS = 64
NY = 8
ROWS = EXPERTS * CAP
STEP = 1024
ORDER = (3, 1, 4, -3, -1, 2, -2, 0)
VMEM = pl.BlockSpec(memory_space=pltpu.VMEM)
F32 = jnp.float32
BF16 = jnp.bfloat16


def gate_kernel(tf_ref, tr_ref, rf_ref, rr_ref, router_ref, own_ref, far_ref, m1_ref, m2_ref, m3_ref, table):
    experts = lax.broadcasted_iota(jnp.int32, (EXPERTS, TOK), 0)
    later = lax.broadcasted_iota(jnp.int32, (TOK, TOK), 0) < lax.broadcasted_iota(jnp.int32, (TOK, TOK), 1)
    later = later.astype(F32).astype(BF16)
    shares, ranks = [], []
    for t_ref, r_ref in ((tf_ref, rf_ref), (tr_ref, rr_ref)):
        logits = lax.dot_general(
            router_ref[...], t_ref[...], (((1,), (1,)), ((), ())), preferred_element_type=F32
        )
        named = jnp.zeros((EXPERTS, TOK), F32)
        for k in range(8):
            named = named + (r_ref[k : k + 1, :] == experts).astype(F32)
        raised = jnp.where(named > 0, jnp.exp(logits), 0.0)
        shares.append(raised / jnp.sum(raised, axis=0, keepdims=True))
        rank = jnp.dot(named.astype(BF16), later, preferred_element_type=F32)
        ranks.append(jnp.where(named > 0, rank, -1.0))
    pad = jnp.zeros((EXPERTS, 128 - 2 * TOK), F32)
    table[:EXPERTS] = jnp.concatenate([*shares, pad], axis=1)
    table[EXPERTS:] = jnp.concatenate([*ranks, pad], axis=1)

    def part(ref, at, offset):
        place = lax.rem(lax.axis_index("y").astype(jnp.int32) + offset, NY)
        ref[at : at + 8] = table[pl.ds(place, 8, stride=NY), :]
        ref[at + 8 : at + 16] = table[pl.ds(EXPERTS + place, 8, stride=NY), :]

    part(own_ref, 0, 0)
    part(far_ref, 0, 4)
    for offset, ref in ((1, m1_ref), (2, m2_ref), (3, m3_ref)):
        part(ref, 0, offset)
        part(ref, 16, offset + 4)


def gate_tables(tf, tr, rf, rr, router_t):
    return pl.pallas_call(
        gate_kernel,
        out_shape=[jax.ShapeDtypeStruct((size, 128), F32) for size in (16, 16, 32, 32, 32)],
        in_specs=[VMEM] * 5,
        out_specs=[VMEM] * 5,
        scratch_shapes=[pltpu.VMEM((2 * EXPERTS, 128), F32)],
        cost_estimate=pl.CostEstimate(flops=2 * 80 * 2048 * 64, bytes_accessed=700_000, transcendentals=5120),
    )(tf, tr, rf, rr, router_t)


def combine_kernel(m, held_ref, m1_ref, m2_ref, m3_ref, far_ref, rows_ref, *outs_and_scratch):
    *outs, weights = outs_and_scratch

    @pl.when(pl.program_id(0) == 0)
    def _():
        y = lax.axis_index("y").astype(jnp.int32)
        column = lax.broadcasted_iota(jnp.int32, (1, ROWS), 1)
        zx = sum((column >= NY * CAP * i).astype(jnp.int32) for i in range(1, EXPERTS // NY))
        column = column - NY * CAP * zx
        dest = sum((column >= CAP * i).astype(jnp.int32) for i in range(1, NY))
        slot = (column - CAP * dest).astype(F32)
        tables = jnp.concatenate([held_ref[64:], m1_ref[:16], m2_ref[:16], m3_ref[:16], far_ref[:64]], axis=0)
        by_token = tables.T[m * TOK : (m + 1) * TOK]
        high = by_token.astype(BF16)
        low = (by_token - high.astype(F32)).astype(BF16)
        behind = (y + NY - dest) & (NY - 1)
        place = lax.broadcasted_iota(jnp.int32, (128, ROWS), 0)
        of_share = (place == behind * 16 + zx).astype(F32).astype(BF16)
        of_rank = (place == behind * 16 + zx + 8).astype(F32).astype(BF16)
        share = jnp.dot(jnp.concatenate([high, low], axis=0), of_share, preferred_element_type=F32)
        mine = jnp.dot(high, of_rank, preferred_element_type=F32) == slot
        share_high = jnp.where(mine, share[:TOK], 0.0)
        share_low = jnp.where(mine, share[TOK:], 0.0)
        there = [dest == lax.rem(y + NY + k, NY) for k in ORDER]
        blocks = [jnp.where(at, part, 0.0) for part in (share_high, share_low) for at in there]
        weights[...] = jnp.concatenate(blocks, axis=0).astype(BF16)

    total = jnp.dot(weights[...], rows_ref[...], preferred_element_type=F32)
    summed = (total[: NY * TOK] + total[NY * TOK :]).astype(BF16)
    at = 0
    for out in outs:
        out[...] = summed[at : at + out.shape[0]]
        at += out.shape[0]


def combine(m, tables, rows):
    width = rows.shape[1]
    sizes = (2 * TOK, TOK, 2 * TOK, 3 * TOK)
    whole = lambda shape: pl.BlockSpec(shape, lambda i: (0,) * len(shape))
    return pl.pallas_call(
        functools.partial(combine_kernel, m),
        grid=(width // STEP,),
        out_shape=[jax.ShapeDtypeStruct((size, width), BF16) for size in sizes],
        in_specs=[
            *[whole(table.shape) for table in tables],
            pl.BlockSpec((ROWS, STEP), lambda i: (0, i)),
        ],
        out_specs=[pl.BlockSpec((size, STEP), lambda i: (0, i)) for size in sizes],
        scratch_shapes=[pltpu.VMEM((2 * NY * TOK, ROWS), BF16)],
        compiler_params=pltpu.CompilerParams(vmem_limit_bytes=32 * 1024 * 1024),
        cost_estimate=pl.CostEstimate(
            flops=4 * NY * TOK * ROWS * width, bytes_accessed=2 * (ROWS + NY * TOK) * width, transcendentals=0
        ),
    )(*tables, rows)


def passed_along(block, axis, distance):
    size = lax.axis_size(axis)
    return lax.ppermute(block, axis, [(i, (i + distance) % size) for i in range(size)])


def halfway(block):
    ns = lax.axis_size("section")
    route = [(s * NY + i, s * NY + (i + (2 if s % 2 == 0 else -2)) % NY) for s in range(ns) for i in range(NY)]
    return lax.ppermute(block, ("section", "y"), route)


def add(*terms):
    total = terms[0].astype(F32)
    for term in terms[1:]:
        total = total + term.astype(F32)
    return total.astype(BF16)


def shards(tf, tr, rf, rr, hf, hr, router, down):
    tokens = (tf[0], tr[0])
    up = lax.axis_index("section") % 2 == 0
    own, far, *sent = gate_tables(tf[0], tr[0], rf[0].T, rr[0].T, router[0].T)
    hf, *sent = lax.optimization_barrier((hf, *sent))
    near = [passed_along(block, "y", 1 + i) for i, block in enumerate(sent)]
    held = jnp.concatenate([far] + [block[16:] for block in near] + [own])
    far = passed_along(held, "y", 4)
    down_w = down[0, 0]
    arrived = []
    for m, hidden in enumerate((hf, hr)):
        rows = jnp.dot(hidden[0, 0], down_w, preferred_element_type=F32).astype(BF16)
        if m == 1:
            rows, far = lax.optimization_barrier((rows, far))
        back = lax.all_to_all(rows, ("zl", "x"), split_axis=0, concat_axis=0, tiled=True)
        ahead31, ahead4, behind31, kept = combine(m, (held, *near, far), back)
        got_ahead = passed_along(ahead31, "y", 1)
        got_four = halfway(ahead4)
        got_behind = passed_along(behind31, "y", -1)
        last_ahead = add(kept[:TOK], got_ahead[:TOK], jnp.where(up, got_four, 0))
        last_behind = add(kept[TOK : 2 * TOK], got_behind[:TOK], jnp.where(up, 0, got_four))
        last_ahead = passed_along(last_ahead, "y", 2)
        last_behind = passed_along(last_behind, "y", -2)
        layer = add(tokens[m], kept[2 * TOK :], got_ahead[TOK:], got_behind[TOK:], last_ahead, last_behind)
        arrived.append(passed_along(layer, "section", 1 - 2 * m)[None])
    return tuple(arrived)


def solution(mesh):
    fine = Mesh(mesh.devices.reshape(8, 2, 4, NY), ("section", "zl", "x", "y"))
    expert = ("zl", "x", "y")
    row = P("section", expert, None)
    block = P("section", expert, None, None)
    return jax.shard_map(
        shards,
        mesh=fine,
        in_specs=(row, row, row, row, block, block, P("section", None, None), block),
        out_specs=(row, row),
        check_vma=False,
    )
```

```python
import functools

import jax
import jax.numpy as jnp
from jax import lax
from jax.experimental import pallas as pl
from jax.experimental.pallas import tpu as pltpu
from jax.sharding import Mesh
from jax.sharding import PartitionSpec as P

TOK = 40
CAP = 7
EXPERTS = 64
NY = 8
ROWS = EXPERTS * CAP
STEP = 2048
ORDER = (3, 1, 4, -3, -1, 2, -2, 0)
VMEM = pl.BlockSpec(memory_space=pltpu.VMEM)
F32 = jnp.float32
BF16 = jnp.bfloat16


def gate_kernel(tf_ref, tr_ref, rf_ref, rr_ref, router_ref, own_ref, far_ref, m1_ref, m2_ref, m3_ref, table):
    experts = lax.broadcasted_iota(jnp.int32, (EXPERTS, TOK), 0)
    later = lax.broadcasted_iota(jnp.int32, (TOK, TOK), 0) < lax.broadcasted_iota(jnp.int32, (TOK, TOK), 1)
    later = later.astype(F32).astype(BF16)
    shares, ranks = [], []
    for t_ref, r_ref in ((tf_ref, rf_ref), (tr_ref, rr_ref)):
        logits = lax.dot_general(
            router_ref[...], t_ref[...], (((1,), (1,)), ((), ())), preferred_element_type=F32
        )
        named = jnp.zeros((EXPERTS, TOK), F32)
        for k in range(8):
            named = named + (r_ref[k : k + 1, :] == experts).astype(F32)
        raised = jnp.where(named > 0, jnp.exp(logits), 0.0)
        shares.append(raised / jnp.sum(raised, axis=0, keepdims=True))
        rank = jnp.dot(named.astype(BF16), later, preferred_element_type=F32)
        ranks.append(jnp.where(named > 0, rank, -1.0))
    pad = jnp.zeros((EXPERTS, 128 - 2 * TOK), F32)
    table[:EXPERTS] = jnp.concatenate([*shares, pad], axis=1)
    table[EXPERTS:] = jnp.concatenate([*ranks, pad], axis=1)

    def part(ref, at, offset):
        place = lax.rem(lax.axis_index("y").astype(jnp.int32) + offset, NY)
        ref[at : at + 8] = table[pl.ds(place, 8, stride=NY), :]
        ref[at + 8 : at + 16] = table[pl.ds(EXPERTS + place, 8, stride=NY), :]

    part(own_ref, 0, 0)
    part(far_ref, 0, 4)
    for offset, ref in ((1, m1_ref), (2, m2_ref), (3, m3_ref)):
        part(ref, 0, offset)
        part(ref, 16, offset + 4)


def gate_tables(tf, tr, rf, rr, router_t):
    return pl.pallas_call(
        gate_kernel,
        out_shape=[jax.ShapeDtypeStruct((size, 128), F32) for size in (16, 16, 32, 32, 32)],
        in_specs=[VMEM] * 5,
        out_specs=[VMEM] * 5,
        scratch_shapes=[pltpu.VMEM((2 * EXPERTS, 128), F32)],
        cost_estimate=pl.CostEstimate(flops=2 * 80 * 2048 * 64, bytes_accessed=700_000, transcendentals=5120),
    )(tf, tr, rf, rr, router_t)


def combine_kernel(m, held_ref, m1_ref, m2_ref, m3_ref, far_ref, rows_ref, *outs_and_scratch):
    *outs, weights = outs_and_scratch

    @pl.when(pl.program_id(0) == 0)
    def _():
        y = lax.axis_index("y").astype(jnp.int32)
        column = lax.broadcasted_iota(jnp.int32, (1, ROWS), 1)
        zx = sum((column >= NY * CAP * i).astype(jnp.int32) for i in range(1, EXPERTS // NY))
        column = column - NY * CAP * zx
        dest = sum((column >= CAP * i).astype(jnp.int32) for i in range(1, NY))
        slot = (column - CAP * dest).astype(F32)
        tables = jnp.concatenate([held_ref[64:], m1_ref[:16], m2_ref[:16], m3_ref[:16], far_ref[:64]], axis=0)
        by_token = tables.T[m * TOK : (m + 1) * TOK]
        high = by_token.astype(BF16)
        low = (by_token - high.astype(F32)).astype(BF16)
        behind = (y + NY - dest) & (NY - 1)
        place = lax.broadcasted_iota(jnp.int32, (128, ROWS), 0)
        of_share = (place == behind * 16 + zx).astype(F32).astype(BF16)
        of_rank = (place == behind * 16 + zx + 8).astype(F32).astype(BF16)
        share = jnp.dot(jnp.concatenate([high, low], axis=0), of_share, preferred_element_type=F32)
        mine = jnp.dot(high, of_rank, preferred_element_type=F32) == slot
        share_high = jnp.where(mine, share[:TOK], 0.0)
        share_low = jnp.where(mine, share[TOK:], 0.0)
        there = [dest == lax.rem(y + NY + k, NY) for k in ORDER]
        blocks = [jnp.where(at, part, 0.0) for part in (share_high, share_low) for at in there]
        weights[...] = jnp.concatenate(blocks, axis=0).astype(BF16)

    total = jnp.dot(weights[...], rows_ref[...], preferred_element_type=F32)
    summed = (total[: NY * TOK] + total[NY * TOK :]).astype(BF16)
    at = 0
    for out in outs:
        out[...] = summed[at : at + out.shape[0]]
        at += out.shape[0]


def combine(m, tables, rows):
    width = rows.shape[1]
    sizes = (2 * TOK, TOK, 2 * TOK, 3 * TOK)
    whole = lambda shape: pl.BlockSpec(shape, lambda i: (0,) * len(shape))
    return pl.pallas_call(
        functools.partial(combine_kernel, m),
        grid=(width // STEP,),
        out_shape=[jax.ShapeDtypeStruct((size, width), BF16) for size in sizes],
        in_specs=[
            *[whole(table.shape) for table in tables],
            pl.BlockSpec((ROWS, STEP), lambda i: (0, i)),
        ],
        out_specs=[pl.BlockSpec((size, STEP), lambda i: (0, i)) for size in sizes],
        scratch_shapes=[pltpu.VMEM((2 * NY * TOK, ROWS), BF16)],
        compiler_params=pltpu.CompilerParams(vmem_limit_bytes=32 * 1024 * 1024),
        cost_estimate=pl.CostEstimate(
            flops=4 * NY * TOK * ROWS * width, bytes_accessed=2 * (ROWS + NY * TOK) * width, transcendentals=0
        ),
    )(*tables, rows)


def passed_along(block, axis, distance):
    size = lax.axis_size(axis)
    return lax.ppermute(block, axis, [(i, (i + distance) % size) for i in range(size)])


def halfway(block):
    ns = lax.axis_size("section")
    route = [(s * NY + i, s * NY + (i + (2 if s % 2 == 0 else -2)) % NY) for s in range(ns) for i in range(NY)]
    return lax.ppermute(block, ("section", "y"), route)


def add(*terms):
    total = terms[0].astype(F32)
    for term in terms[1:]:
        total = total + term.astype(F32)
    return total.astype(BF16)


def shards(tf, tr, rf, rr, hf, hr, router, down):
    tokens = (tf[0], tr[0])
    up = lax.axis_index("section") % 2 == 0
    own, far, *sent = gate_tables(tf[0], tr[0], rf[0].T, rr[0].T, router[0].T)
    hf, *sent = lax.optimization_barrier((hf, *sent))
    near = [passed_along(block, "y", 1 + i) for i, block in enumerate(sent)]
    held = jnp.concatenate([far] + [block[16:] for block in near] + [own])
    far = passed_along(held, "y", 4)
    down_w = down[0, 0]
    arrived = []
    for m, hidden in enumerate((hf, hr)):
        rows = jnp.dot(hidden[0, 0], down_w, preferred_element_type=F32).astype(BF16)
        if m == 1:
            rows, far = lax.optimization_barrier((rows, far))
        back = lax.all_to_all(rows, ("zl", "x"), split_axis=0, concat_axis=0, tiled=True)
        ahead31, ahead4, behind31, kept = combine(m, (held, *near, far), back)
        got_ahead = passed_along(ahead31, "y", 1)
        got_four = halfway(ahead4)
        got_behind = passed_along(behind31, "y", -1)
        last_ahead = add(kept[:TOK], got_ahead[:TOK], jnp.where(up, got_four, 0))
        last_behind = add(kept[TOK : 2 * TOK], got_behind[:TOK], jnp.where(up, 0, got_four))
        last_ahead = passed_along(last_ahead, "y", 2)
        last_behind = passed_along(last_behind, "y", -2)
        layer = add(tokens[m], kept[2 * TOK :], got_ahead[TOK:], got_behind[TOK:], last_ahead, last_behind)
        arrived.append(passed_along(layer, "section", 1 - 2 * m)[None])
    return tuple(arrived)


def solution(mesh):
    fine = Mesh(mesh.devices.reshape(8, 2, 4, NY), ("section", "zl", "x", "y"))
    expert = ("zl", "x", "y")
    row = P("section", expert, None)
    block = P("section", expert, None, None)
    return jax.shard_map(
        shards,
        mesh=fine,
        in_specs=(row, row, row, row, block, block, P("section", None, None), block),
        out_specs=(row, row),
        check_vma=False,
    )
```
